32 devices in a mesh: rows: 8 (over z, y), cols: 4 (over x, core).
Axes of the slice: x: 2, y: 2, z: 4, core: 2. Of those that a mesh axis runs over, the one named last changes fastest.
Arguments:
- features: bfloat16 [256, 1024], P('cols', 'rows'), may hold values from -6 to 6
- weight_matrix: bfloat16 [256, 256], replicated, may hold values from -0.375 to 0.375
- bias_vector: float32 [256], replicated, may hold values from -3 to 3
- adjacency_tiles: bfloat16 [8, 5, 128, 128], P('rows')
- tile_cols: int32 [8, 5], P('rows'), may hold values from 0 to 7, as said below
- tile_count: int32 [8], P('rows'), may hold values from 3 to 5, as said below
- out_grad: bfloat16 [256, 1024], P('cols', 'rows'), may hold values from -6 to 6
Outputs:
- layer_out: bfloat16 [256, 1024], P('cols', 'rows')
- feature_grad: bfloat16 [256, 1024], P('cols', 'rows')
- weight_grad: float32 [256, 256], P('cols')
- bias_grad: float32 [256], P('cols')
The draws below stay inside these ranges and needn't reach their ends.
Inputs may be any that keep to these rules, and one draw needn't show every extreme that they name: `tile_cols`: the live slots of a row block name distinct column blocks, its own among them; the pattern is symmetric: c is live in row block b exactly when b is live in row block c, and that tile is the transpose of the one of b in c's list. Slots past tile_count hold the row block's own index. Outside the hub's row, every live column block other than the hub lies within 1 block of the row block around the cycle of 8 blocks; the hub's own row also holds such band blocks. `tile_count`: exactly one row block, the hub, has all 5 slots live.
All inputs are finite; a program needn't handle non-finite values.
Results may differ from the reference program's by a relative error of at most 0.008.
Values may be sent and summed in bfloat16 or wider, within the bound.
A program may use at most 64 MiB of HBM per device.

```python
import math
import jax
import jax.numpy as jnp
from jax import lax

F = 256
BLK = 128
NB = 8
NEAR = 1
BAND = 1
HUBS = 1
TPR = 5
NODES = 1024


def tile_pattern(key):
    base_key = jax.random.fold_in(key, 11)
    near_offsets = (jax.random.permutation(jax.random.fold_in(base_key, 1), BAND)[:NEAR] + 1).astype(jnp.int32)
    candidate = jax.random.permutation(jax.random.fold_in(base_key, 3), NB - 2 * BAND - 2)[:2 * HUBS - 1].astype(jnp.int32) + BAND + 1
    candidate = jnp.where(candidate >= NB // 2, candidate + 1, candidate).astype(jnp.int32)
    far_dists = jnp.concatenate([jnp.full((1,), NB // 2, jnp.int32), candidate]).astype(jnp.int32)
    hub_block = jax.random.randint(jax.random.fold_in(base_key, 2), (), 0, NB).astype(jnp.int32)
    block_index = jnp.arange(NB, dtype=jnp.int32)
    base_cols = jnp.concatenate([block_index[:, None], (block_index[:, None] + near_offsets[None, :]) % NB, (block_index[:, None] - near_offsets[None, :] + NB) % NB], axis=1)
    hub_cols = (hub_block + far_dists) % NB
    distance = (block_index - hub_block + NB) % NB
    partner = jnp.any(distance[:, None] == far_dists[None, :], axis=1)
    is_hub = block_index == hub_block
    first_extra = jnp.where(is_hub, hub_cols[0], jnp.where(partner, hub_block, block_index))
    extra_cols = jnp.where(is_hub[:, None], hub_cols[None, :], jnp.broadcast_to(block_index[:, None], (NB, 2 * HUBS)))
    extra_cols = extra_cols.at[:, 0].set(first_extra)
    column_ids = jnp.concatenate([base_cols, extra_cols], axis=1).astype(jnp.int32)
    live_count = 2 * NEAR + 1 + jnp.where(is_hub, 2 * HUBS, partner.astype(jnp.int32))
    return (column_ids, live_count.astype(jnp.int32))


def draw_tile_cols(key, part):
    return tile_pattern(key)[0]


def draw_tile_count(key, part):
    return tile_pattern(key)[1]


def draw_adjacency_tiles(key, part):
    column_ids, live_count = tile_pattern(key)
    row_blocks = jnp.broadcast_to(jnp.arange(NB, dtype=jnp.int32)[:, None], (NB, TPR))
    slot_index = jnp.broadcast_to(jnp.arange(TPR, dtype=jnp.int32)[None, :], (NB, TPR))
    pair_low = jnp.minimum(row_blocks, column_ids)
    pair_high = jnp.maximum(row_blocks, column_ids)
    alive = slot_index < live_count[:, None]
    pair_number = jnp.where(alive, pair_low * NB + pair_high, NB * NB + row_blocks * TPR + slot_index)
    value_key = jax.random.fold_in(key, 23)
    sigma = (BLK * (2 * NEAR + 1)) ** (-0.5)

    def draw_pair(number):
        pair_rng = jax.random.fold_in(value_key, number)
        return jax.random.normal(pair_rng, (BLK, BLK), jnp.float32)
    matrices = jax.vmap(draw_pair)(pair_number.reshape(-1)).reshape(NB, TPR, BLK, BLK)
    swapped = jnp.swapaxes(matrices, 2, 3)
    symmetric = (matrices + swapped) * 0.5 ** 0.5
    diagonal = (row_blocks == column_ids)[:, :, None, None]
    flipped = (row_blocks > column_ids)[:, :, None, None]
    values = jnp.where(diagonal, symmetric, jnp.where(flipped, swapped, matrices)) * sigma
    return values.astype(jnp.bfloat16)


def block_scale(own_key, shape, cuts, smallest, top_value):
    def one(position, blocks):
        draws = jax.random.uniform(jax.random.fold_in(jax.random.fold_in(own_key, 6), position), (blocks,), jnp.float32, smallest / len(cuts), top_value / len(cuts))
        return jnp.repeat(jnp.exp(draws), shape[position] // blocks).reshape((-1,) + (1,) * (len(shape) - position - 1))

    gain = one(*cuts[0])
    for cut in cuts[1:]:
        gain = gain * one(*cut)
    return gain


def scatter_about(rng, shape, deviation, most, pieces=(), held_as=jnp.bfloat16):
    drawn = deviation * jax.random.normal(rng, shape, jnp.float32)
    if pieces:
        drawn = drawn * block_scale(rng, shape, pieces, -0.22, 0.18)
    return jnp.clip(drawn, -most, most).astype(held_as)


def setup_inputs(seed: int = 0) -> dict:
    seeds = jax.random.split(jax.random.key(seed), 8)
    features = scatter_about(seeds[0], (F, NODES), 1.0, 6.0, ((0, 4), (1, 8)))
    weight_matrix = scatter_about(seeds[1], (F, F), F ** -0.5, 0.375)
    bias_vector = scatter_about(seeds[2], (F,), 0.5, 3.0, (), jnp.float32)
    adjacency_tiles = draw_adjacency_tiles(jax.random.fold_in(seeds[7], 71), 0)
    tile_cols = draw_tile_cols(jax.random.fold_in(seeds[7], 71), 0)
    tile_count = draw_tile_count(jax.random.fold_in(seeds[7], 71), 0)
    out_grad = scatter_about(seeds[6], (F, NODES), 1.0, 6.0, ((0, 4), (1, 8)))
    return dict(features=features, weight_matrix=weight_matrix, bias_vector=bias_vector, adjacency_tiles=adjacency_tiles, tile_cols=tile_cols, tile_count=tile_count, out_grad=out_grad)


def reference(features, weight_matrix, bias_vector, adjacency_tiles, tile_cols, tile_count, out_grad):
    block_view = features.reshape(F, NB, BLK)
    slot_index = jnp.arange(TPR, dtype=jnp.int32)
    alive_mask = slot_index[None, :] < tile_count[:, None]

    def forward_block(inputs):
        tile_set, column_ids, alive = inputs
        panel = jnp.take(block_view, column_ids, axis=1).astype(jnp.float32)
        panel = panel * alive[None, :, None].astype(jnp.float32)
        return jnp.einsum('fsk,srk->fr', panel, tile_set.astype(jnp.float32))
    aggregated = lax.map(forward_block, (adjacency_tiles, tile_cols, alive_mask))
    aggregated = aggregated.transpose(1, 0, 2).reshape(F, NODES).astype(jnp.bfloat16)
    preact = jnp.dot(weight_matrix, aggregated, preferred_element_type=jnp.float32) + bias_vector[:, None]
    sigmoid_pre = jax.nn.sigmoid(preact)
    layer_out = (preact * sigmoid_pre).astype(jnp.bfloat16)
    pre_grad = (out_grad.astype(jnp.float32) * sigmoid_pre * (1.0 + preact * (1.0 - sigmoid_pre))).astype(jnp.bfloat16)
    grad_scale = 1.0 / math.sqrt(NODES)
    weight_grad = jnp.dot(pre_grad, aggregated.T, preferred_element_type=jnp.float32) * grad_scale
    bias_grad = lax.optimization_barrier(jnp.sum(pre_grad.astype(jnp.float32), axis=1)) * grad_scale
    agg_grad = jnp.dot(weight_matrix.T, pre_grad, preferred_element_type=jnp.float32).astype(jnp.bfloat16)
    grad_blocks = agg_grad.reshape(F, NB, BLK).transpose(1, 0, 2)

    def adjoint_step(running, inputs):
        tile_set, column_ids, alive, own_block = inputs
        contrib = jnp.einsum('fr,srk->sfk', own_block.astype(jnp.float32), tile_set.astype(jnp.float32))
        contrib = contrib * alive[:, None, None].astype(jnp.float32)
        return (running.at[column_ids].add(contrib), None)
    running = jnp.zeros((NB, F, BLK), jnp.float32)
    running = lax.scan(adjoint_step, running, (adjacency_tiles, tile_cols, alive_mask, grad_blocks))[0]
    feature_grad = running.transpose(1, 0, 2).reshape(F, NODES).astype(jnp.bfloat16)
    return (layer_out, feature_grad, weight_grad, bias_grad)
```

```python
import functools
import math

import jax
import jax.numpy as jnp
from jax import lax
from jax.experimental import pallas as pl
from jax.experimental.pallas import tpu as pltpu
from jax.sharding import PartitionSpec as P

MESH = pl.DeviceIdType.MESH
NT = (((1,), (1,)), ((), ()))
NN = (((1,), (0,)), ((), ()))


def mm(a, b, dims=NN):
    return lax.dot_general(a, b, dims, preferred_element_type=jnp.float32)


def loop(low, high, body):
    if high - low <= 16:
        for i in range(low, high):
            body(i)
    else:
        pl.loop(low, high)(body)


def kernel(
    nr, nc, scale,
    f_hbm, w_hbm, b_hbm, a_hbm, tc_hbm, tn_hbm, og_hbm,
    lo_out, fg_out, wg_out, bg_out,
    panel, gpan, aggf, ogf, w, wt, bvec, bmat, adj, tc, tn, pg, lo, wpart, rs, wfull, bpart,
    lsem, f_s, f_r, o_s, o_r, a_s, a_r, g_s, g_r, b_s, b_r, w_s, w_r, v_s, v_r,
):
    r, c = lax.axis_index("rows"), lax.axis_index("cols")
    nb, fl, side = panel.shape
    bh, slots = adj.shape[:2]
    chunk = rs.shape[1]
    reducers = fl // chunk

    def row_peer(d):
        return lax.rem(r + d, nr)

    def col_peer(d):
        return lax.rem(c + d, nc)

    local = [
        pltpu.make_async_copy(
            f_hbm.at[:, pl.ds(i * side, side)], panel.at[r * bh + i], lsem.at[7 + i]
        )
        for i in range(bh)
    ]
    mine = pl.ds(pl.multiple_of(c * fl, fl), fl)
    og_local = pltpu.make_async_copy(og_hbm, ogf.at[mine], lsem.at[0])
    w_local = pltpu.make_async_copy(w_hbm, w, lsem.at[1])
    b_local = pltpu.make_async_copy(b_hbm, bvec, lsem.at[2])
    a_local = pltpu.make_async_copy(a_hbm, adj, lsem.at[3])
    tc_local = pltpu.make_async_copy(tc_hbm, tc, lsem.at[4])
    tn_local = pltpu.make_async_copy(tn_hbm, tn, lsem.at[5])
    for cp in local + [og_local, w_local, b_local, tc_local, tn_local, a_local]:
        cp.start()

    barrier = pltpu.get_barrier_semaphore()

    def hello_row(d):
        pl.semaphore_signal(barrier, 1, device_id={"rows": row_peer(d)}, device_id_type=MESH)

    def hello_col(d):
        pl.semaphore_signal(barrier, 1, device_id={"cols": col_peer(d)}, device_id_type=MESH)

    loop(1, nr, hello_row)
    loop(1, nc, hello_col)
    for cp in local:
        cp.wait()
    og_local.wait()
    pl.semaphore_wait(barrier, nr + nc - 2)

    own = pl.ds(r * bh, bh)

    def row_copy(src, dst, s, t, d):
        return pltpu.make_async_remote_copy(
            src_ref=src, dst_ref=dst, send_sem=s.at[d], recv_sem=t.at[d],
            device_id={"rows": row_peer(d)}, device_id_type=MESH,
        )

    def col_copy(src, dst, s, t, d):
        return pltpu.make_async_remote_copy(
            src_ref=src, dst_ref=dst, send_sem=s.at[d], recv_sem=t.at[d],
            device_id={"cols": col_peer(d)}, device_id_type=MESH,
        )

    def f_copy(d):
        return row_copy(panel.at[own], panel.at[own], f_s, f_r, d)

    def o_copy(d):
        return col_copy(ogf.at[mine], ogf.at[mine], o_s, o_r, d)

    def a_copy(d):
        return col_copy(aggf.at[mine], aggf.at[mine], a_s, a_r, d)

    def g_copy(d):
        return row_copy(gpan.at[own], gpan.at[own], g_s, g_r, d)

    def b_copy(d):
        return row_copy(bpart.at[r], bpart.at[r], b_s, b_r, d)

    def w_copy(d):
        src = wpart.at[pl.ds(pl.multiple_of(row_peer(d) * chunk, chunk), chunk)]
        return row_copy(src, rs.at[r], w_s, w_r, d)

    def w_copy_in(d):
        return row_copy(rs.at[r], rs.at[r], w_s, w_r, d)

    my_chunk = pl.ds(pl.multiple_of(r * chunk, chunk), chunk)

    def v_copy(d):
        return row_copy(wfull.at[my_chunk], wfull.at[my_chunk], v_s, v_r, d)

    def v_copy_in(d):
        return row_copy(wfull.at[pl.ds(0, chunk)], wfull.at[pl.ds(0, chunk)], v_s, v_r, d)

    loop(1, nr, lambda d: f_copy(d).start())
    loop(1, nc, lambda d: o_copy(d).start())

    w_local.wait()
    wt[...] = w[...].T
    b_local.wait()
    bmat[...] = jnp.broadcast_to(bvec[...], (side, bvec.shape[1])).T
    tc_local.wait()
    tn_local.wait()
    a_local.wait()

    def products(pan, i):
        def one(s, acc):
            term = mm(pan[tc[i, s]], adj[i, s], NT)
            return acc + jnp.where(s < tn[i], term, 0.0)

        acc = jnp.zeros((fl, side), jnp.float32)
        if slots <= 8:
            for s in range(slots):
                acc = one(s, acc)
            return acc
        return lax.fori_loop(0, slots, one, acc)

    loop(1, nr, lambda d: f_copy(d).wait_recv())
    for i in range(bh):
        aggf[mine, pl.ds(i * side, side)] = products(panel, i).astype(jnp.bfloat16)
    loop(1, nc, lambda d: a_copy(d).start())
    loop(1, nc, lambda d: o_copy(d).wait_recv())
    loop(1, nc, lambda d: a_copy(d).wait_recv())

    for i in range(bh):
        at = pl.ds(i * side, side)
        pre = mm(w[...], aggf[:, at]) + bmat[...]
        sig = jax.nn.sigmoid(pre)
        lo[:, at] = (pre * sig).astype(jnp.bfloat16)
        pg[:, at] = (
            ogf[:, at].astype(jnp.float32) * sig * (1.0 + pre * (1.0 - sig))
        ).astype(jnp.bfloat16)

    wpart[...] = mm(pg[mine, :], aggf[...], NT)

    def w_send(d):
        if reducers == nr:
            w_copy(d).start()
        else:
            pl.when(row_peer(d) < reducers)(lambda: w_copy(d).start())

    loop(1, nr, w_send)
    for i in range(bh):
        gpan[r * bh + i] = mm(wt[mine, :], pg[:, pl.ds(i * side, side)]).astype(jnp.bfloat16)
    loop(1, nr, lambda d: g_copy(d).start())
    ones = jnp.ones((8, bh * side), jnp.bfloat16)
    bpart[r] = mm(ones, pg[mine, :], NT)
    loop(1, nr, lambda d: b_copy(d).start())
    lo_out[...] = lo[mine, :]

    def reduce_chunk():
        loop(1, nr, lambda d: w_copy_in(d).wait_recv())
        rs[r] = wpart[my_chunk, :]
        total = rs[0]
        if nr <= 16:
            for k in range(1, nr):
                total = total + rs[k]
        else:
            total = lax.fori_loop(1, nr, lambda k, t: t + rs[k], total)
        wfull[my_chunk, :] = total * scale
        loop(1, nr, lambda d: v_copy(d).start())

    if reducers == nr:
        reduce_chunk()
    else:
        pl.when(r < reducers)(reduce_chunk)

    loop(1, nr, lambda d: g_copy(d).wait_recv())
    for i in range(bh):
        fg_out[:, pl.ds(i * side, side)] = products(gpan, i).astype(jnp.bfloat16)

    loop(1, nr, lambda d: b_copy(d).wait_recv())
    btot = bpart[0]
    for k in range(1, nr):
        btot = btot + bpart[k]
    bg_out[...] = btot[0:1, :] * scale

    def v_wait(d):
        if reducers == nr:
            v_copy_in(d).wait_recv()
        else:
            pl.when(lax.rem(r - d + nr, nr) < reducers)(lambda: v_copy_in(d).wait_recv())

    loop(1, nr, v_wait)
    wg_out[...] = wfull[...]

    def w_done(d):
        if reducers == nr:
            w_copy(d).wait_send()
        else:
            pl.when(row_peer(d) < reducers)(lambda: w_copy(d).wait_send())

    def v_done(d):
        if reducers == nr:
            v_copy(d).wait_send()
        else:
            pl.when(r < reducers)(lambda: v_copy(d).wait_send())

    loop(1, nr, lambda d: f_copy(d).wait_send())
    loop(1, nc, lambda d: o_copy(d).wait_send())
    loop(1, nc, lambda d: a_copy(d).wait_send())
    loop(1, nr, lambda d: g_copy(d).wait_send())
    loop(1, nr, lambda d: b_copy(d).wait_send())
    loop(1, nr, w_done)
    loop(1, nr, v_done)


def per_device(nr, nc, features, weight_matrix, bias_vector, adjacency_tiles, tile_cols, tile_count, out_grad):
    fl, nodes = features.shape
    bh, slots = tile_cols.shape
    side = adjacency_tiles.shape[-1]
    full = weight_matrix.shape[0]
    nb = bh * nr
    bf, f32 = jnp.bfloat16, jnp.float32
    chunk = max(8, fl // nr)
    scale = 1.0 / math.sqrt(nodes * nr)
    vmem, dma = pltpu.VMEM, pltpu.SemaphoreType.DMA
    any_spec = pl.BlockSpec(memory_space=pl.ANY)
    out_spec = pl.BlockSpec(memory_space=pltpu.VMEM)
    lo, fg, wg, bg = pl.pallas_call(
        functools.partial(kernel, nr, nc, scale),
        out_shape=(
            jax.ShapeDtypeStruct((fl, nodes), bf),
            jax.ShapeDtypeStruct((fl, nodes), bf),
            jax.ShapeDtypeStruct((fl, full), f32),
            jax.ShapeDtypeStruct((1, fl), f32),
        ),
        in_specs=[any_spec] * 7,
        out_specs=(out_spec,) * 4,
        scratch_shapes=[
            vmem((nb, fl, side), bf),
            vmem((nb, fl, side), bf),
            vmem((full, nodes), bf),
            vmem((full, nodes), bf),
            vmem((full, full), bf),
            vmem((full, full), bf),
            vmem((1, full), f32),
            vmem((full, side), f32),
            vmem((bh, slots, side, side), bf),
            pltpu.SMEM((bh, slots), jnp.int32),
            pltpu.SMEM((bh,), jnp.int32),
            vmem((full, nodes), bf),
            vmem((full, nodes), bf),
            vmem((fl, full), f32),
            vmem((nr, chunk, full), f32),
            vmem((fl, full), f32),
            vmem((nr, 8, fl), f32),
            dma((7 + bh,)),
            dma((nr,)), dma((nr,)),
            dma((nc,)), dma((nc,)),
            dma((nc,)), dma((nc,)),
            dma((nr,)), dma((nr,)),
            dma((nr,)), dma((nr,)),
            dma((nr,)), dma((nr,)),
            dma((nr,)), dma((nr,)),
        ],
        compiler_params=pltpu.CompilerParams(
            collective_id=0, has_side_effects=True, vmem_limit_bytes=40 * 1024 * 1024
        ),
    )(
        features, weight_matrix, bias_vector.reshape(1, full), adjacency_tiles,
        tile_cols, tile_count, out_grad,
    )
    return lo, fg, wg, bg.reshape(fl)


def solution(mesh):
    return jax.shard_map(
        functools.partial(per_device, mesh.shape["rows"], mesh.shape["cols"]),
        mesh=mesh,
        in_specs=(
            P("cols", "rows"),
            P(),
            P(),
            P("rows", None, None, None),
            P("rows", None),
            P("rows"),
            P("cols", "rows"),
        ),
        out_specs=(P("cols", "rows"), P("cols", "rows"), P("cols", None), P("cols")),
        check_vma=False,
    )
```

```python
import functools
import math

import jax
import jax.numpy as jnp
from jax import lax
from jax.experimental import pallas as pl
from jax.experimental.pallas import tpu as pltpu
from jax.sharding import PartitionSpec as P

MESH = pl.DeviceIdType.MESH
NT = (((1,), (1,)), ((), ()))
NN = (((1,), (0,)), ((), ()))


def mm(a, b, dims=NN):
    return lax.dot_general(a, b, dims, preferred_element_type=jnp.float32)


def is_static(count):
    return count <= 16 and count & (count - 1) == 0


def loop(low, high, body):
    if is_static(high):
        for i in sorted(range(low, high), key=lambda d: -((d ^ (d >> 1)) + (d & high // 2) * high)):
            body(i)
    else:
        pl.loop(low, high)(body)


def partner(me, d, count):
    if not is_static(count):
        return lax.rem(me + d, count)
    other, bit = me, 1
    while bit < count:
        if d & bit:
            other = other + bit - 2 * bit * lax.rem(lax.div(me, bit), 2)
        bit *= 2
    return other


def stack_halves(x, side):
    return jnp.concatenate(
        [x[:, h * side : (h + 1) * side] for h in range(x.shape[1] // side)], axis=0
    )


def kernel(
    nr, nc, scale,
    f_hbm, w_hbm, b_hbm, a_hbm, tc_hbm, tn_hbm, og_hbm,
    lo_out, fg_out, wg_out, bg_out,
    panel, gpan, aggf, ogf, w, wt, bvec, bmat, adj, tc, tn, pg, lo, wpart, rs, wfull,
    lsem, f_s, f_r, o_s, o_r, a_s, a_r, g_s, g_r, w_s, w_r, v_s, v_r,
):
    r, c = lax.axis_index("rows"), lax.axis_index("cols")
    nb, fl, side = panel.shape
    bh, slots = adj.shape[:2]
    reducers = wpart.shape[0]
    chunk = fl // reducers
    parts = w.shape[0] // side

    def row_peer(d):
        return partner(r, d, nr)

    def col_peer(d):
        return partner(c, d, nc)

    barrier = pltpu.get_barrier_semaphore()

    def hello_row(d):
        pl.semaphore_signal(barrier, 1, device_id={"rows": row_peer(d)}, device_id_type=MESH)

    def hello_col(d):
        pl.semaphore_signal(barrier, 1, device_id={"cols": col_peer(d)}, device_id_type=MESH)

    loop(1, nr, hello_row)
    loop(1, nc, hello_col)

    local = [
        pltpu.make_async_copy(
            f_hbm.at[:, pl.ds(i * side, side)], panel.at[r * bh + i], lsem.at[7 + i]
        )
        for i in range(bh)
    ]
    mine = pl.ds(pl.multiple_of(c * fl, fl), fl)
    og_local = pltpu.make_async_copy(og_hbm, ogf.at[mine], lsem.at[0])
    w_local = pltpu.make_async_copy(w_hbm, w, lsem.at[1])
    b_local = pltpu.make_async_copy(b_hbm, bvec, lsem.at[2])
    a_local = pltpu.make_async_copy(a_hbm, adj, lsem.at[3])
    tc_local = pltpu.make_async_copy(tc_hbm, tc, lsem.at[4])
    tn_local = pltpu.make_async_copy(tn_hbm, tn, lsem.at[5])
    for cp in local + [og_local, w_local, b_local, tc_local, tn_local, a_local]:
        cp.start()
    for cp in local:
        cp.wait()
    og_local.wait()
    pl.semaphore_wait(barrier, nr + nc - 2)

    own = pl.ds(r * bh, bh)

    def row_copy(src, dst, s, t, d):
        return pltpu.make_async_remote_copy(
            src_ref=src, dst_ref=dst, send_sem=s.at[d], recv_sem=t.at[d],
            device_id={"rows": row_peer(d)}, device_id_type=MESH,
        )

    def col_copy(src, dst, s, t, d):
        return pltpu.make_async_remote_copy(
            src_ref=src, dst_ref=dst, send_sem=s.at[d], recv_sem=t.at[d],
            device_id={"cols": col_peer(d)}, device_id_type=MESH,
        )

    def f_copy(d):
        return row_copy(panel.at[own], panel.at[own], f_s, f_r, d)

    def o_copy(d):
        return col_copy(ogf.at[mine], ogf.at[mine], o_s, o_r, d)

    def a_copy(d):
        return col_copy(aggf.at[mine], aggf.at[mine], a_s, a_r, d)

    def g_copy(d):
        return row_copy(gpan.at[own], gpan.at[own], g_s, g_r, d)

    def w_copy(d):
        return row_copy(wpart.at[row_peer(d)], rs.at[r], w_s, w_r, d)

    def w_copy_in(d):
        return row_copy(rs.at[r], rs.at[r], w_s, w_r, d)

    def v_copy(d):
        return row_copy(wfull.at[r], wfull.at[r], v_s, v_r, d)

    def v_copy_in(d):
        return row_copy(wfull.at[0], wfull.at[0], v_s, v_r, d)

    loop(1, nr, lambda d: f_copy(d).start())
    loop(1, nc, lambda d: o_copy(d).start())

    w_local.wait()
    wt[...] = w[...].T
    b_local.wait()
    bmat[...] = jnp.broadcast_to(bvec[...], (side, bvec.shape[1])).T
    tc_local.wait()
    tn_local.wait()
    a_local.wait()

    def products(pan, i):
        def one(s, acc):
            term = mm(pan[tc[i, s], pl.ds(0, fl), :], adj[i, s], NT)
            return acc + jnp.where(s < tn[i], term, 0.0)

        acc = jnp.zeros((fl, side), jnp.float32)
        if slots <= 8:
            for s in range(slots):
                acc = one(s, acc)
            return acc
        return lax.fori_loop(0, slots, one, acc)

    loop(1, nr, lambda d: f_copy(d).wait_recv())
    for i in range(bh):
        aggf[mine, pl.ds(i * side, side)] = products(panel, i).astype(jnp.bfloat16)
    loop(1, nc, lambda d: a_copy(d).start())
    loop(1, nc, lambda d: o_copy(d).wait_recv())
    loop(1, nc, lambda d: a_copy(d).wait_recv())

    for i in range(bh):
        at = pl.ds(i * side, side)
        pre = mm(w[...], aggf[:, at]) + bmat[...]
        sig = jax.nn.sigmoid(pre)
        lo[:, at] = (pre * sig).astype(jnp.bfloat16)
        pg[:, at] = (
            ogf[:, at].astype(jnp.float32) * sig * (1.0 + pre * (1.0 - sig))
        ).astype(jnp.bfloat16)

    wgrad = mm(pg[mine, :], aggf[...], NT)
    for j in range(reducers):
        wpart[j] = stack_halves(wgrad[j * chunk : (j + 1) * chunk, :], side).astype(jnp.bfloat16)

    def w_send(d):
        if reducers == nr:
            w_copy(d).start()
        else:
            pl.when(row_peer(d) < reducers)(lambda: w_copy(d).start())

    loop(1, nr, w_send)
    for i in range(bh):
        at = pl.ds(i * side, side)
        gpan[r * bh + i, pl.ds(0, fl), :] = mm(wt[mine, :], pg[:, at]).astype(jnp.bfloat16)
        total = mm(jnp.ones((16, side), jnp.bfloat16), pg[mine, at], NT)
        high = total.astype(jnp.bfloat16).astype(jnp.float32)
        middle = (total - high).astype(jnp.bfloat16).astype(jnp.float32)
        line = lax.broadcasted_iota(jnp.int32, total.shape, 0)
        rest = jnp.where(line == 2, total - high - middle, 0.0)
        digits = jnp.where(line == 0, high, jnp.where(line == 1, middle, rest))
        gpan[r * bh + i, pl.ds(fl, 16), pl.ds(0, fl)] = digits.astype(jnp.bfloat16)
    loop(1, nr, lambda d: g_copy(d).start())
    lo_out[...] = lo[mine, :]

    def reduce_chunk():
        loop(1, nr, lambda d: w_copy_in(d).wait_recv())
        rs[r] = wpart[r]
        total = rs[0].astype(jnp.float32)
        if nr <= 16:
            for k in range(1, nr):
                total = total + rs[k].astype(jnp.float32)
        else:
            total = lax.fori_loop(1, nr, lambda k, t: t + rs[k].astype(jnp.float32), total)
        wfull[r] = (total * scale).astype(jnp.bfloat16)
        loop(1, nr, lambda d: v_copy(d).start())

    if reducers == nr:
        reduce_chunk()
    else:
        pl.when(r < reducers)(reduce_chunk)

    loop(1, nr, lambda d: g_copy(d).wait_recv())
    for i in range(bh):
        fg_out[:, pl.ds(i * side, side)] = products(gpan, i).astype(jnp.bfloat16)

    def bias_rows(k):
        return gpan[k, pl.ds(fl, 16), pl.ds(0, fl)].astype(jnp.float32)

    btot = bias_rows(0)
    for k in range(1, nb):
        btot = btot + bias_rows(k)
    bg_out[...] = jnp.sum(btot, axis=0, keepdims=True) * scale

    def v_wait(d):
        if reducers == nr:
            v_copy_in(d).wait_recv()
        else:
            pl.when(lax.rem(r - d + nr, nr) < reducers)(lambda: v_copy_in(d).wait_recv())

    loop(1, nr, v_wait)
    for j in range(reducers):
        piece = wfull[j].astype(jnp.float32)
        for h in range(parts):
            wg_out[pl.ds(j * chunk, chunk), pl.ds(h * side, side)] = piece[h * chunk : (h + 1) * chunk, :]

    def w_done(d):
        if reducers == nr:
            w_copy(d).wait_send()
        else:
            pl.when(row_peer(d) < reducers)(lambda: w_copy(d).wait_send())

    def v_done(d):
        if reducers == nr:
            v_copy(d).wait_send()
        else:
            pl.when(r < reducers)(lambda: v_copy(d).wait_send())

    loop(1, nr, lambda d: f_copy(d).wait_send())
    loop(1, nc, lambda d: o_copy(d).wait_send())
    loop(1, nc, lambda d: a_copy(d).wait_send())
    loop(1, nr, lambda d: g_copy(d).wait_send())
    loop(1, nr, w_done)
    loop(1, nr, v_done)


def write_out(*refs):
    copies = [
        pltpu.make_async_copy(refs[i], refs[4 + i], refs[8].at[i]) for i in range(4)
    ]
    for cp in copies:
        cp.start()
    for cp in copies:
        cp.wait()


def per_device(nr, nc, features, weight_matrix, bias_vector, adjacency_tiles, tile_cols, tile_count, out_grad):
    fl, nodes = features.shape
    bh, slots = tile_cols.shape
    side = adjacency_tiles.shape[-1]
    full = weight_matrix.shape[0]
    nb = bh * nr
    bf, f32 = jnp.bfloat16, jnp.float32
    chunk = max(8, fl // nr)
    piece = (chunk * full // side, side)
    scale = 1.0 / math.sqrt(nodes * nr)
    vmem, dma = pltpu.VMEM, pltpu.SemaphoreType.DMA
    hbm_spec = pl.BlockSpec(memory_space=pltpu.HBM)
    any_spec = pl.BlockSpec(memory_space=pl.ANY)
    out_spec = pl.BlockSpec(memory_space=pltpu.VMEM)
    results = (
        jax.ShapeDtypeStruct((fl, nodes), bf),
        jax.ShapeDtypeStruct((fl, nodes), bf),
        jax.ShapeDtypeStruct((fl, full), f32),
        jax.ShapeDtypeStruct((1, fl), f32),
    )
    held = pl.pallas_call(
        functools.partial(kernel, nr, nc, scale),
        out_shape=results,
        in_specs=[hbm_spec] * 7,
        out_specs=(out_spec,) * 4,
        scratch_shapes=[
            vmem((nb, fl, side), bf),
            vmem((nb, fl + 16, side), bf),
            vmem((full, nodes), bf),
            vmem((full, nodes), bf),
            vmem((full, full), bf),
            vmem((full, full), bf),
            vmem((1, full), f32),
            vmem((full, side), f32),
            vmem((bh, slots, side, side), bf),
            pltpu.SMEM((bh, slots), jnp.int32),
            pltpu.SMEM((bh,), jnp.int32),
            vmem((full, nodes), bf),
            vmem((full, nodes), bf),
            vmem((fl // chunk,) + piece, bf),
            vmem((nr,) + piece, bf),
            vmem((fl // chunk,) + piece, bf),
            dma((7 + bh,)),
            dma((nr,)), dma((nr,)),
            dma((nc,)), dma((nc,)),
            dma((nc,)), dma((nc,)),
            dma((nr,)), dma((nr,)),
            dma((nr,)), dma((nr,)),
            dma((nr,)), dma((nr,)),
        ],
        compiler_params=pltpu.CompilerParams(
            collective_id=0, has_side_effects=True, vmem_limit_bytes=63 * 1024 * 1024
        ),
    )(
        features, weight_matrix, bias_vector.reshape(1, full), adjacency_tiles,
        tile_cols, tile_count, out_grad,
    )
    lo, fg, wg, bg = pl.pallas_call(
        write_out,
        out_shape=results,
        in_specs=[out_spec] * 4,
        out_specs=(hbm_spec,) * 4,
        scratch_shapes=[dma((4,))], compiler_params=pltpu.CompilerParams(vmem_limit_bytes=63 * 1024 * 1024),
    )(*held)
    return lo, fg, wg, bg.reshape(fl)


def solution(mesh):
    return jax.shard_map(
        functools.partial(per_device, mesh.shape["rows"], mesh.shape["cols"]),
        mesh=mesh,
        in_specs=(
            P("cols", "rows"),
            P(),
            P(),
            P("rows", None, None, None),
            P("rows", None),
            P("rows"),
            P("cols", "rows"),
        ),
        out_specs=(P("cols", "rows"), P("cols", "rows"), P("cols", None), P("cols")),
        check_vma=False,
    )
```

```python
import functools
import math

import jax
import jax.numpy as jnp
from jax import lax
from jax.experimental import pallas as pl
from jax.experimental.pallas import tpu as pltpu
from jax.sharding import PartitionSpec as P

MESH = pl.DeviceIdType.MESH
NT = (((1,), (1,)), ((), ()))
NN = (((1,), (0,)), ((), ()))


def mm(a, b, dims=NN):
    return lax.dot_general(a, b, dims, preferred_element_type=jnp.float32)


def is_static(count):
    return count <= 16 and count & (count - 1) == 0


def loop(low, high, body):
    if is_static(high):
        for i in sorted(range(low, high), key=lambda d: -((d ^ (d >> 1)) + (d & high // 2) * high)):
            body(i)
    else:
        pl.loop(low, high)(body)


def partner(me, d, count):
    if not is_static(count):
        return lax.rem(me + d, count)
    other, bit = me, 1
    while bit < count:
        if d & bit:
            other = other + bit - 2 * bit * lax.rem(lax.div(me, bit), 2)
        bit *= 2
    return other


def stack_halves(x, side):
    return jnp.concatenate(
        [x[:, h * side : (h + 1) * side] for h in range(x.shape[1] // side)], axis=0
    )


def kernel(
    nr, nc, scale,
    f_hbm, w_hbm, b_hbm, a_hbm, tc_hbm, tn_hbm, og_hbm,
    lo_out, fg_out, wg_out, bg_out,
    panel, gpan, aggf, ogf, w, wt, bvec, bmat, adj, tc, tn, pg, lo, wpart, rs, wfull,
    lsem, f_s, f_r, o_s, o_r, a_s, a_r, g_s, g_r, w_s, w_r, v_s, v_r,
):
    r, c = lax.axis_index("rows"), lax.axis_index("cols")
    nb, fl, side = panel.shape
    bh, slots = adj.shape[:2]
    reducers = wpart.shape[0]
    chunk = fl // reducers

    def row_peer(d):
        return partner(r, d, nr)

    def col_peer(d):
        return partner(c, d, nc)

    barrier = pltpu.get_barrier_semaphore()

    def hello_row(d):
        pl.semaphore_signal(barrier, 1, device_id={"rows": row_peer(d)}, device_id_type=MESH)

    def hello_col(d):
        pl.semaphore_signal(barrier, 1, device_id={"cols": col_peer(d)}, device_id_type=MESH)

    loop(1, nr, hello_row)
    loop(1, nc, hello_col)

    local = [
        pltpu.make_async_copy(
            f_hbm.at[:, pl.ds(i * side, side)], panel.at[r * bh + i], lsem.at[7 + i]
        )
        for i in range(bh)
    ]
    mine = pl.ds(pl.multiple_of(c * fl, fl), fl)
    og_local = pltpu.make_async_copy(og_hbm, ogf.at[mine], lsem.at[0])
    w_local = pltpu.make_async_copy(w_hbm, w, lsem.at[1])
    b_local = pltpu.make_async_copy(b_hbm, bvec, lsem.at[2])
    a_local = pltpu.make_async_copy(a_hbm, adj, lsem.at[3])
    tc_local = pltpu.make_async_copy(tc_hbm, tc, lsem.at[4])
    tn_local = pltpu.make_async_copy(tn_hbm, tn, lsem.at[5])
    for cp in local + [og_local, w_local, b_local, tc_local, tn_local, a_local]:
        cp.start()
    for cp in local:
        cp.wait()
    og_local.wait()
    pl.semaphore_wait(barrier, nr + nc - 2)

    own = pl.ds(r * bh, bh)

    def row_copy(src, dst, s, t, d):
        return pltpu.make_async_remote_copy(
            src_ref=src, dst_ref=dst, send_sem=s.at[d], recv_sem=t.at[d],
            device_id={"rows": row_peer(d)}, device_id_type=MESH,
        )

    def col_copy(src, dst, s, t, d):
        return pltpu.make_async_remote_copy(
            src_ref=src, dst_ref=dst, send_sem=s.at[d], recv_sem=t.at[d],
            device_id={"cols": col_peer(d)}, device_id_type=MESH,
        )

    def f_copy(d):
        return row_copy(panel.at[own], panel.at[own], f_s, f_r, d)

    def o_copy(d):
        return col_copy(ogf.at[mine], ogf.at[mine], o_s, o_r, d)

    def a_copy(d):
        return col_copy(aggf.at[mine], aggf.at[mine], a_s, a_r, d)

    def g_copy(d):
        return row_copy(gpan.at[own], gpan.at[own], g_s, g_r, d)

    def w_copy(d):
        return row_copy(wpart.at[row_peer(d)], rs.at[r], w_s, w_r, d)

    def w_copy_in(d):
        return row_copy(rs.at[r], rs.at[r], w_s, w_r, d)

    def v_copy(d):
        return row_copy(wfull.at[r], wfull.at[r], v_s, v_r, d)

    def v_copy_in(d):
        return row_copy(wfull.at[0], wfull.at[0], v_s, v_r, d)

    loop(1, nr, lambda d: f_copy(d).start())
    loop(1, nc, lambda d: o_copy(d).start())

    w_local.wait()
    wt[...] = w[...].T
    b_local.wait()
    bmat[...] = jnp.broadcast_to(bvec[...], (side, bvec.shape[1])).T
    tc_local.wait()
    tn_local.wait()
    a_local.wait()

    def products(pan, i):
        def one(s, acc):
            term = mm(pan[tc[i, s], pl.ds(0, fl), :], adj[i, s], NT)
            return acc + jnp.where(s < tn[i], term, 0.0)

        acc = jnp.zeros((fl, side), jnp.float32)
        if slots <= 8:
            for s in range(slots):
                acc = one(s, acc)
            return acc
        return lax.fori_loop(0, slots, one, acc)

    loop(1, nr, lambda d: f_copy(d).wait_recv())
    for i in range(bh):
        aggf[mine, pl.ds(i * side, side)] = products(panel, i).astype(jnp.bfloat16)
    loop(1, nc, lambda d: a_copy(d).start())
    loop(1, nc, lambda d: o_copy(d).wait_recv())
    loop(1, nc, lambda d: a_copy(d).wait_recv())

    for i in range(bh):
        at = pl.ds(i * side, side)
        pre = mm(w[...], aggf[:, at]) + bmat[...]
        sig = jax.nn.sigmoid(pre)
        lo[:, at] = (pre * sig).astype(jnp.bfloat16)
        pg[:, at] = (
            ogf[:, at].astype(jnp.float32) * sig * (1.0 + pre * (1.0 - sig))
        ).astype(jnp.bfloat16)

    wgrad = mm(pg[mine, :], aggf[...], NT)
    for j in range(reducers):
        wpart[j] = stack_halves(wgrad[j * chunk : (j + 1) * chunk, :], side).astype(jnp.bfloat16)

    def w_send(d):
        if reducers == nr:
            w_copy(d).start()
        else:
            pl.when(row_peer(d) < reducers)(lambda: w_copy(d).start())

    loop(1, nr, w_send)
    for i in range(bh):
        at = pl.ds(i * side, side)
        gpan[r * bh + i, pl.ds(0, fl), :] = mm(wt[mine, :], pg[:, at]).astype(jnp.bfloat16)
        total = mm(jnp.ones((16, side), jnp.bfloat16), pg[mine, at], NT)
        high = total.astype(jnp.bfloat16).astype(jnp.float32)
        middle = (total - high).astype(jnp.bfloat16).astype(jnp.float32)
        line = lax.broadcasted_iota(jnp.int32, total.shape, 0)
        rest = jnp.where(line == 2, total - high - middle, 0.0)
        digits = jnp.where(line == 0, high, jnp.where(line == 1, middle, rest))
        gpan[r * bh + i, pl.ds(fl, 16), pl.ds(0, fl)] = digits.astype(jnp.bfloat16)
    loop(1, nr, lambda d: g_copy(d).start())
    lo_out[...] = lo[mine, :]

    def reduce_chunk():
        loop(1, nr, lambda d: w_copy_in(d).wait_recv())
        rs[r] = wpart[r]
        total = rs[0].astype(jnp.float32)
        if nr <= 16:
            for k in range(1, nr):
                total = total + rs[k].astype(jnp.float32)
        else:
            total = lax.fori_loop(1, nr, lambda k, t: t + rs[k].astype(jnp.float32), total)
        wfull[r] = (total * scale).astype(jnp.bfloat16)
        loop(1, nr, lambda d: v_copy(d).start())

    if reducers == nr:
        reduce_chunk()
    else:
        pl.when(r < reducers)(reduce_chunk)

    loop(1, nr, lambda d: g_copy(d).wait_recv())
    for i in range(bh):
        fg_out[:, pl.ds(i * side, side)] = products(gpan, i).astype(jnp.bfloat16)

    def bias_rows(k):
        return gpan[k, pl.ds(fl, 16), pl.ds(0, fl)].astype(jnp.float32)

    btot = bias_rows(0)
    for k in range(1, nb):
        btot = btot + bias_rows(k)
    bg_out[...] = jnp.sum(btot, axis=0, keepdims=True) * scale

    def v_wait(d):
        if reducers == nr:
            v_copy_in(d).wait_recv()
        else:
            pl.when(lax.rem(r - d + nr, nr) < reducers)(lambda: v_copy_in(d).wait_recv())

    loop(1, nr, v_wait)
    wg_out[...] = wfull[...]

    def w_done(d):
        if reducers == nr:
            w_copy(d).wait_send()
        else:
            pl.when(row_peer(d) < reducers)(lambda: w_copy(d).wait_send())

    def v_done(d):
        if reducers == nr:
            v_copy(d).wait_send()
        else:
            pl.when(r < reducers)(lambda: v_copy(d).wait_send())

    loop(1, nr, lambda d: f_copy(d).wait_send())
    loop(1, nc, lambda d: o_copy(d).wait_send())
    loop(1, nc, lambda d: a_copy(d).wait_send())
    loop(1, nr, lambda d: g_copy(d).wait_send())
    loop(1, nr, w_done)
    loop(1, nr, v_done)


def write_out(*refs):
    copies = [
        pltpu.make_async_copy(refs[i], refs[4 + i], refs[8].at[i]) for i in (0, 1, 3)
    ]
    for cp in copies:
        cp.start()
    held, wg_out = refs[2], refs[6]
    side = held.shape[2]
    chunk = wg_out.shape[0] // held.shape[0]
    for j in range(held.shape[0]):
        piece = held[j].astype(jnp.float32)
        for h in range(wg_out.shape[1] // side):
            wg_out[pl.ds(j * chunk, chunk), pl.ds(h * side, side)] = piece[h * chunk : (h + 1) * chunk, :]
    for cp in copies:
        cp.wait()


def per_device(nr, nc, features, weight_matrix, bias_vector, adjacency_tiles, tile_cols, tile_count, out_grad):
    fl, nodes = features.shape
    bh, slots = tile_cols.shape
    side = adjacency_tiles.shape[-1]
    full = weight_matrix.shape[0]
    nb = bh * nr
    bf, f32 = jnp.bfloat16, jnp.float32
    chunk = max(8, fl // nr)
    piece = (chunk * full // side, side)
    scale = 1.0 / math.sqrt(nodes * nr)
    vmem, dma = pltpu.VMEM, pltpu.SemaphoreType.DMA
    hbm_spec = pl.BlockSpec(memory_space=pltpu.HBM)
    any_spec = pl.BlockSpec(memory_space=pl.ANY)
    out_spec = pl.BlockSpec(memory_space=pltpu.VMEM)
    results = (
        jax.ShapeDtypeStruct((fl, nodes), bf),
        jax.ShapeDtypeStruct((fl, nodes), bf),
        jax.ShapeDtypeStruct((fl, full), f32),
        jax.ShapeDtypeStruct((1, fl), f32),
    )
    held = pl.pallas_call(
        functools.partial(kernel, nr, nc, scale),
        out_shape=results[:2] + (jax.ShapeDtypeStruct((fl // chunk,) + piece, bf), results[3]),
        in_specs=[hbm_spec] * 7,
        out_specs=(out_spec,) * 4,
        scratch_shapes=[
            vmem((nb, fl, side), bf),
            vmem((nb, fl + 16, side), bf),
            vmem((full, nodes), bf),
            vmem((full, nodes), bf),
            vmem((full, full), bf),
            vmem((full, full), bf),
            vmem((1, full), f32),
            vmem((full, side), f32),
            vmem((bh, slots, side, side), bf),
            pltpu.SMEM((bh, slots), jnp.int32),
            pltpu.SMEM((bh,), jnp.int32),
            vmem((full, nodes), bf),
            vmem((full, nodes), bf),
            vmem((fl // chunk,) + piece, bf),
            vmem((nr,) + piece, bf),
            vmem((fl // chunk,) + piece, bf),
            dma((7 + bh,)),
            dma((nr,)), dma((nr,)),
            dma((nc,)), dma((nc,)),
            dma((nc,)), dma((nc,)),
            dma((nr,)), dma((nr,)),
            dma((nr,)), dma((nr,)),
            dma((nr,)), dma((nr,)),
        ],
        compiler_params=pltpu.CompilerParams(
            collective_id=0, has_side_effects=True, vmem_limit_bytes=63 * 1024 * 1024
        ),
    )(
        features, weight_matrix, bias_vector.reshape(1, full), adjacency_tiles,
        tile_cols, tile_count, out_grad,
    )
    lo, fg, wg, bg = pl.pallas_call(
        write_out,
        out_shape=results,
        in_specs=[out_spec] * 4,
        out_specs=(hbm_spec, hbm_spec, out_spec, hbm_spec),
        scratch_shapes=[dma((4,))], compiler_params=pltpu.CompilerParams(vmem_limit_bytes=63 * 1024 * 1024),
    )(*held)
    return lo, fg, wg, bg.reshape(fl)


def solution(mesh):
    return jax.shard_map(
        functools.partial(per_device, mesh.shape["rows"], mesh.shape["cols"]),
        mesh=mesh,
        in_specs=(
            P("cols", "rows"),
            P(),
            P(),
            P("rows", None, None, None),
            P("rows", None),
            P("rows"),
            P("cols", "rows"),
        ),
        out_specs=(P("cols", "rows"), P("cols", "rows"), P("cols", None), P("cols")),
        check_vma=False,
    )
```
